32 devices in a mesh: left: 4 (over x, core), right: 8 (over z, y).
Axes of the slice: x: 2, y: 2, z: 4, core: 2. Of those that a mesh axis runs over, the one named last changes fastest.
Arguments:
- left_table: bfloat16 [8192, 256], P('left'), may hold values from -1.5 to 1.5
- right_table: bfloat16 [4, 4096, 256], P('left', 'right'), may hold values from -1.5 to 1.5
- relations: float32 [512, 256], replicated, may hold values from -6 to 6
- source_ids: int32 [4, 8, 1024], P('left', 'right'), may hold values from 0 to 2047
- relation_ids: int32 [4, 8, 1024], P('left', 'right'), may hold values from 0 to 511
- target_ids: int32 [4, 8, 1024], P('left', 'right'), may hold values from 0 to 511
- negative_ids: int32 [4, 8, 1, 1024], P('left', 'right'), may hold values from 0 to 511
- edge_counts: int32 [4, 8], P('left', 'right'), may hold values from 1 to 1024
Outputs:
- left_next: bfloat16 [8192, 256], P('left')
- right_next: bfloat16 [4, 4096, 256], P('left', 'right')
- relations_next: float32 [512, 256], replicated
The draws below stay inside these ranges and needn't reach their ends.
Inputs may be any that keep to these rules, and one draw needn't show every extreme that they name: Edge slots at positions from edge_counts to 1023 hold ids but are padding.
All inputs are finite; a program needn't handle non-finite values.
Results may differ from the reference program's by a relative error of at most 0.0013.
Values may be sent and summed in bfloat16 or wider, within the bound.
A program may use at most 64 MiB of HBM per device.

```python
import math
import jax
import jax.numpy as jnp
import numpy as np
from jax import lax

D = 256
REL = 512
NEG = 1024
GROUP = 1024
GROUPS = 1
ENT_L = 2048
ENT_R = 512
EDGE_CAP = 1024
LEFT_PARTS = 4
RIGHT_PARTS = 8
LEFT_ROWS = 8192
RIGHT_ROWS = 4096
N_LEFT = 4
N_RIGHT = 8


def touch_ends(entries, stream_key, least, top_value):
    place = [jax.random.randint(jax.random.fold_in(stream_key, axis), (), 0, length) for axis, length in enumerate(entries.shape)]
    widest = entries.shape.index(max(entries.shape))
    neighbour = place[:widest] + [(place[widest] + 1) % entries.shape[widest]] + place[widest + 1:]
    return entries.at[tuple(place)].set(least).at[tuple(neighbour)].set(top_value)


def block_levels(rng, extent, shards, smallest, largest):
    def one(dim, parts):
        draws = jax.random.uniform(jax.random.fold_in(jax.random.fold_in(rng, 6), dim), (parts,), jnp.float32, smallest / len(shards), largest / len(shards))
        return jnp.repeat(jnp.exp(draws), extent[dim] // parts).reshape((-1,) + (1,) * (len(extent) - dim - 1))

    gain = one(*shards[0])
    for cut in shards[1:]:
        gain = gain * one(*cut)
    return gain


def rank_table(amount, slope):
    weights = [(1 << 20) // math.isqrt(rank ** slope) + 1 for rank in range(1, amount + 1)]
    spread = 1 + sum(weights) // (1 << 30)
    return np.cumsum(np.array([max(1, weight // spread) for weight in weights]))


def ranked_ids(own_key, dims, amount, slope):
    grid = rank_table(amount, slope)
    pick = jax.random.randint(jax.random.fold_in(own_key, 1), dims, 0, int(grid[amount - 1]))
    grade = jnp.searchsorted(jnp.asarray(grid, jnp.int32), pick, side="right")
    return jax.random.permutation(jax.random.fold_in(own_key, 2), amount)[grade].astype(jnp.int32)


def gaussian(stream_key, dims, deviation, bound, pieces=(), kind=jnp.bfloat16):
    result = deviation * jax.random.normal(stream_key, dims, jnp.float32)
    if pieces:
        result = result * block_levels(stream_key, dims, pieces, -0.22, 0.18)
    return jnp.clip(result, -bound, bound).astype(kind)


def setup_inputs(seed: int = 0) -> dict:
    splits = jax.random.split(jax.random.key(seed), 9)
    return {
        "left_table": gaussian(splits[0], (LEFT_ROWS, D), 0.25, 1.5, ((0, 4),)),
        "right_table": gaussian(splits[1], (LEFT_PARTS, RIGHT_ROWS, D), 0.25, 1.5, ((0, 4), (1, 8))),
        "relations": gaussian(splits[2], (REL, D), 1.0, 6.0, (), jnp.float32),
        "source_ids": touch_ends(jax.random.randint(splits[3], (LEFT_PARTS, RIGHT_PARTS, EDGE_CAP), 0, ENT_L), jax.random.fold_in(splits[3], 1), 0, ENT_L - 1).astype(jnp.int32),
        "relation_ids": touch_ends(ranked_ids(splits[4], (LEFT_PARTS, RIGHT_PARTS, EDGE_CAP), REL, 2), jax.random.fold_in(splits[4], 3), 0, REL - 1).astype(jnp.int32),
        "target_ids": touch_ends(jax.random.randint(splits[5], (LEFT_PARTS, RIGHT_PARTS, EDGE_CAP), 0, ENT_R), jax.random.fold_in(splits[5], 1), 0, ENT_R - 1).astype(jnp.int32),
        "negative_ids": touch_ends(jax.random.randint(splits[6], (LEFT_PARTS, RIGHT_PARTS, GROUPS, NEG), 0, ENT_R), jax.random.fold_in(splits[6], 1), 0, ENT_R - 1).astype(jnp.int32),
        "edge_counts": touch_ends(jax.random.randint(splits[7], (LEFT_PARTS, RIGHT_PARTS), 1, EDGE_CAP + 1), jax.random.fold_in(splits[7], 1), 1, EDGE_CAP).astype(jnp.int32),
    }


step_size = 0.5
relation_step = 12.0


def block_terms(left_blk, right_blk, relations, src, kind, dst, neg, live):
    half = relations.shape[1] // 2
    head = left_blk[src].astype(jnp.float32)
    tail = right_blk[dst].astype(jnp.float32)
    rel = relations[kind]
    hre, him = head[:, :half], head[:, half:]
    rre, rim = rel[:, :half], rel[:, half:]
    query = jnp.concatenate([hre * rre - him * rim, hre * rim + him * rre], axis=1)
    q_low = query.astype(jnp.bfloat16)
    pos = jnp.sum(query * tail, axis=1)
    negrows = right_blk[neg]
    scores = jnp.dot(q_low, negrows.T, preferred_element_type=jnp.float32)
    c_pos = -jax.nn.sigmoid(-pos) * live
    c_neg = (jax.nn.sigmoid(scores) * (live[:, None] / neg.shape[0])).astype(jnp.bfloat16)
    g_query = jnp.dot(c_neg, negrows, preferred_element_type=jnp.float32) + c_pos[:, None] * tail
    g_neg = jnp.dot(c_neg.T, q_low, preferred_element_type=jnp.float32)
    g_tail = c_pos[:, None] * query
    gre, gim = g_query[:, :half], g_query[:, half:]
    grad_h = jnp.concatenate([gre * rre + gim * rim, -gre * rim + gim * rre], axis=1)
    grad_r = jnp.concatenate([gre * hre + gim * him, -gre * him + gim * hre], axis=1)
    return grad_h, grad_r, g_tail, g_neg


def bucket(left_blk, right_blk, relations, src, kind, dst, negs, count):
    def one(carry, index):
        lgrad, rgrad, tgrad = carry
        start = index * GROUP
        s = lax.dynamic_slice_in_dim(src, start, GROUP)
        k = lax.dynamic_slice_in_dim(kind, start, GROUP)
        d = lax.dynamic_slice_in_dim(dst, start, GROUP)
        n = negs[index]
        live = ((start + jnp.arange(GROUP, dtype=jnp.int32)) < count).astype(jnp.float32)
        grad_h, grad_r, g_tail, g_neg = block_terms(left_blk, right_blk, relations, s, k, d, n, live)
        lgrad = lgrad.at[s].add(grad_h)
        rgrad = rgrad.at[k].add(grad_r)
        tgrad = tgrad.at[d].add(g_tail).at[n].add(g_neg)
        return (lgrad, rgrad, tgrad), None
    init = (jnp.zeros(left_blk.shape, jnp.float32), jnp.zeros(relations.shape, jnp.float32), jnp.zeros(right_blk.shape, jnp.float32))
    out, unused = lax.scan(one, init, jnp.arange(GROUPS, dtype=jnp.int32))
    return out


def reference(left_table, right_table, relations, source_ids, relation_ids, target_ids, negative_ids, edge_counts):
    lefts = left_table.reshape(N_LEFT, ENT_L, D)
    rights = right_table.reshape(N_LEFT, N_RIGHT, ENT_R, D)

    def per_left(items):
        left_blk, right_row, src_row, kind_row, dst_row, neg_row, count_row = items

        def per_bucket(carry, xs):
            lsum, rsum = carry
            right_blk, src, kind, dst, negs, count = xs
            lgrad, rgrad, tgrad = bucket(left_blk, right_blk, relations, src, kind, dst, negs, count)
            updated = (right_blk.astype(jnp.float32) - step_size * tgrad).astype(jnp.bfloat16)
            return (lsum + lgrad, rsum + rgrad), updated
        init = (jnp.zeros((ENT_L, D), jnp.float32), jnp.zeros((REL, D), jnp.float32))
        (lsum, rsum), updated = lax.scan(per_bucket, init, (right_row, src_row, kind_row, dst_row, neg_row, count_row))
        new_left = (left_blk.astype(jnp.float32) - step_size * lsum).astype(jnp.bfloat16)
        return new_left, rsum, updated

    new_lefts, rel_parts, updated = lax.map(per_left, (lefts, rights, source_ids, relation_ids, target_ids, negative_ids, edge_counts))
    rel_total = jnp.sum(rel_parts, axis=0)
    right_next = jnp.roll(updated, 1, axis=1).reshape(N_LEFT, N_RIGHT * ENT_R, D)
    relations_next = relations - relation_step * rel_total
    return new_lefts.reshape(N_LEFT * ENT_L, D), right_next, relations_next
```

```python
import functools

import jax
import jax.numpy as jnp
from jax import lax
from jax.experimental import pallas as pl
from jax.experimental.pallas import tpu as pltpu
from jax.sharding import PartitionSpec as P

step_size = 0.5
relation_step = 12.0

f32, bf16 = jnp.float32, jnp.bfloat16
VMEM = pltpu.VMEM


def split(value):
    high = value.astype(bf16)
    low = (value - high.astype(f32)).astype(bf16)
    return jnp.concatenate([high, low], axis=1)


def joined(value):
    half = value.shape[1] // 2
    return value[:, :half] + value[:, half:]


def matmul(a, b, dims=((1,), (0,))):
    return lax.dot_general(a, b, (dims, ((), ())), preferred_element_type=f32)


def one_hot(ids, shape, axis):
    place = lax.broadcasted_iota(jnp.int32, shape, axis)
    return jnp.where(place == ids, 1.0, 0.0).astype(bf16)


def terms_kernel(
    count_ref, left_ref, right_ref, rel_ref, src_ref, kind_ref, dst_ref, neg_ref,
    lgrad_ref, rgrad_ref, updated_ref,
    rows_ref, cols_ref, rel_parts, neg_parts, heads, kinds, tails, low_ref, weights,
):
    edges = src_ref.shape[1]
    ent_l, width = left_ref.shape
    ent_r = right_ref.shape[0]
    rels = rel_ref.shape[0]
    negs = neg_ref.shape[1]
    half = width // 2
    block = min(256, edges)

    rows_ref[...] = jnp.zeros_like(rows_ref)
    rows_ref[0:1, :] = src_ref[...]
    rows_ref[1:2, :] = kind_ref[...]
    rows_ref[2:3, :] = dst_ref[...]
    cols_ref[...] = jnp.transpose(rows_ref[...])
    rel_parts[...] = split(rel_ref[...])
    place = lax.broadcasted_iota(jnp.int32, (ent_r, negs), 0)
    times = jnp.sum(jnp.where(place == neg_ref[...], 1.0, 0.0), axis=1, keepdims=True)
    neg_parts[...] = split(right_ref[...].astype(f32) * times)
    count = count_ref[0, 0]

    @pl.loop(0, edges // block)
    def _(step):
        start = pl.multiple_of(step * block, block)
        here = pl.ds(start, block)
        ids = cols_ref[here, :]
        head = matmul(one_hot(ids[:, 0:1], (block, ent_l), 1), left_ref[...])
        rel = joined(matmul(one_hot(ids[:, 1:2], (block, rels), 1), rel_parts[...]))
        tail = matmul(one_hot(ids[:, 2:3], (block, ent_r), 1), right_ref[...])
        slot = start + lax.broadcasted_iota(jnp.int32, (block, 1), 0)
        live = jnp.where(slot < count, 1.0, 0.0)
        hre, him = head[:, :half], head[:, half:]
        rre, rim = rel[:, :half], rel[:, half:]
        query = jnp.concatenate([hre * rre - him * rim, hre * rim + him * rre], axis=1)
        q_low = query.astype(bf16)
        pos = jnp.sum(query * tail, axis=1, keepdims=True)
        scores = matmul(q_low, right_ref[...], ((1,), (1,)))
        c_pos = -live / (1.0 + jnp.exp(pos))
        c_neg = ((live / negs) / (1.0 + jnp.exp(-scores))).astype(bf16)
        g_query = joined(matmul(c_neg, neg_parts[...])) + c_pos * tail
        gre, gim = g_query[:, :half], g_query[:, half:]
        heads[here, :] = split(
            jnp.concatenate([gre * rre + gim * rim, -gre * rim + gim * rre], axis=1)
        )
        kinds[here, :] = split(
            jnp.concatenate([gre * hre + gim * him, -gre * him + gim * hre], axis=1)
        )
        tails[here, :] = split(c_pos * query)
        low_ref[here, :] = q_low
        weights[here, :] = c_neg

    def summed(ids_row, rows, parts, store):
        size = min(256, rows)

        @pl.loop(0, rows // size)
        def _(step):
            start = pl.multiple_of(step * size, size)
            hot = one_hot(ids_row[...] - start, (size, edges), 0)
            store(start, size, joined(matmul(hot, parts[...])))

    def store_left(start, size, value):
        lgrad_ref[pl.ds(start, size), :] = value

    def store_rel(start, size, value):
        rgrad_ref[pl.ds(start, size), :] = value

    grad = matmul(weights[...], low_ref[...], ((0,), (0,))) * times
    hot = one_hot(dst_ref[...], (ent_r, edges), 0)
    grad = grad + joined(matmul(hot, tails[...]))
    updated_ref[...] = (right_ref[...].astype(f32) - step_size * grad).astype(bf16)
    summed(kind_ref, rels, kinds, store_rel)
    summed(src_ref, ent_l, heads, store_left)


def terms(left, right, relations, src, kind, dst, neg, count):
    edges = src.shape[1]
    ent_l, width = left.shape
    ent_r, rels = right.shape[0], relations.shape[0]
    whole = pl.BlockSpec(memory_space=VMEM)
    return pl.pallas_call(
        terms_kernel,
        out_shape=(
            jax.ShapeDtypeStruct((ent_l, width), f32),
            jax.ShapeDtypeStruct((rels, width), f32),
            jax.ShapeDtypeStruct((ent_r, width), bf16),
        ),
        in_specs=[pl.BlockSpec(memory_space=pltpu.SMEM)] + [whole] * 7,
        out_specs=(whole,) * 3,
        scratch_shapes=[
            VMEM((8, edges), jnp.int32),
            VMEM((edges, 8), jnp.int32),
            VMEM((rels, 2 * width), bf16),
            VMEM((ent_r, 2 * width), bf16),
            VMEM((edges, 2 * width), bf16),
            VMEM((edges, 2 * width), bf16),
            VMEM((edges, 2 * width), bf16),
            VMEM((edges, width), bf16),
            VMEM((edges, ent_r), bf16),
        ],
        compiler_params=pltpu.CompilerParams(vmem_limit_bytes=44 * 2**20),
        name="bucket_terms",
    )(count, left, right, relations, src, kind, dst, neg)


def exchange_kernel(
    nl, nr,
    lgrad_ref, rgrad_ref, block_ref, left_ref, rel_ref,
    left_out, block_out, rel_out,
    pair_in, line_in, rel_in, rel_mid, rel_part,
    block_sems, pair_send, pair_recv, line_send, line_recv,
    rows_send, rows_recv, back_send, back_recv,
    ra_send, ra_recv, rb_send, rb_recv, rc_send, rc_recv, rd_send, rd_recv,
):
    m = nr // 2
    l, r = lax.axis_index("left"), lax.axis_index("right")
    line, side = r // 2, lax.rem(r, 2)
    mate = line * 2 + (1 - side)

    def across(src, dst, send, recv, axis, to):
        return pltpu.make_async_remote_copy(
            src_ref=src, dst_ref=dst, send_sem=send, recv_sem=recv,
            device_id={axis: to}, device_id_type=pl.DeviceIdType.MESH,
        )

    def others(me, count):
        return [lax.rem(me + k, count) for k in range(1, count)]

    lefts, rights, lines = others(l, nl), others(r, nr), others(line, m)

    barrier = pltpu.get_barrier_semaphore()
    for axis, peers in (("left", lefts), ("right", rights)):
        for peer in peers:
            pl.semaphore_signal(
                barrier, inc=1, device_id={axis: peer},
                device_id_type=pl.DeviceIdType.MESH,
            )
    pl.semaphore_wait(barrier, nl - 1 + nr - 1)

    started = []

    def start(*what):
        copy = across(*what)
        copy.start()
        started.append(copy)

    for peer in lefts:
        start(rgrad_ref.at[peer], rel_in.at[l], ra_send.at[peer], ra_recv.at[l], "left", peer)
    order = lines + [line]
    for j in order:
        start(
            lgrad_ref.at[1 - side, j], pair_in.at[j], pair_send.at[j], pair_recv.at[j],
            "right", mate,
        )
    after = lax.rem(r + 1, nr)
    start(block_ref, block_out, block_sems.at[0], block_sems.at[1], "right", after)

    def arrived(dst, sem, axis="right"):
        across(dst, dst, sem, sem, axis, mate if axis == "right" else lefts[0]).wait_recv()

    total = rgrad_ref[l]
    for peer in lefts:
        arrived(rel_in.at[peer], ra_recv.at[peer], "left")
        total = total + rel_in[peer]
    rel_part[...] = total
    for peer in rights:
        start(rel_part.at[peer], rel_mid.at[r], rb_send.at[peer], rb_recv.at[r], "right", peer)

    for j in order:
        arrived(pair_in.at[j], pair_recv.at[j])
        pair_in[j] = pair_in[j] + lgrad_ref[side, j]
        if j is not line:
            start(
                pair_in.at[j], line_in.at[line], line_send.at[j], line_recv.at[line],
                "right", j * 2 + side,
            )

    total = rel_part[r]
    for peer in rights:
        arrived(rel_mid.at[peer], rb_recv.at[peer])
        total = total + rel_mid[peer]
    rel_out[l, r] = rel_ref[l, r] - relation_step * total
    for peer in rights:
        start(rel_out.at[l, r], rel_out.at[l, r], rc_send.at[peer], rc_recv.at[r], "right", peer)

    total = pair_in[line]
    for j in lines:
        arrived(line_in.at[j], line_recv.at[j])
        total = total + line_in[j]
    left_out[side, line] = (
        left_ref[side, line].astype(f32) - step_size * total
    ).astype(bf16)
    own = left_out.at[side, line]
    for j in lines:
        start(own, own, rows_send.at[j], rows_recv.at[line], "right", j * 2 + side)
    start(own, own, back_send.at[line], back_recv.at[line], "right", mate)

    for peer in rights:
        arrived(rel_out.at[l, peer], rc_recv.at[peer])
    for peer in lefts:
        start(rel_out.at[l], rel_out.at[l], rd_send.at[peer], rd_recv.at[l], "left", peer)

    for j in lines:
        piece = left_out.at[side, j]
        arrived(piece, rows_recv.at[j])
        start(piece, piece, back_send.at[j], back_recv.at[j], "right", mate)
    for j in order:
        arrived(left_out.at[1 - side, j], back_recv.at[j])
    for peer in lefts:
        arrived(rel_out.at[peer], rd_recv.at[peer], "left")
    arrived(block_out, block_sems.at[1])
    for copy in started:
        copy.wait_send()


def exchange(nl, nr, lgrad, rgrad, block, left, relations):
    m = nr // 2
    ent_l, width = left.shape
    rels = relations.shape[0]
    piece, part, share = ent_l // nr, rels // nl, rels // (nl * nr)
    whole = pl.BlockSpec(memory_space=VMEM)
    dma = pltpu.SemaphoreType.DMA
    left_next, moved, relations_next = pl.pallas_call(
        functools.partial(exchange_kernel, nl, nr),
        out_shape=(
            jax.ShapeDtypeStruct((2, m, piece, width), bf16),
            jax.ShapeDtypeStruct(block.shape, bf16),
            jax.ShapeDtypeStruct((nl, nr, share, width), f32),
        ),
        in_specs=[whole] * 5,
        out_specs=(whole,) * 3,
        scratch_shapes=[
            VMEM((m, piece, width), f32),
            VMEM((m, piece, width), f32),
            VMEM((nl, nr, share, width), f32),
            VMEM((nr, share, width), f32),
            VMEM((nr, share, width), f32),
            dma((2,)),
        ] + [dma((m,))] * 8 + [dma((nl,))] * 2 + [dma((nr,))] * 4 + [dma((nl,))] * 2,
        compiler_params=pltpu.CompilerParams(
            collective_id=0, has_side_effects=True, vmem_limit_bytes=44 * 2**20
        ),
        name="exchange",
    )(
        lgrad.reshape(2, m, piece, width),
        rgrad.reshape(nl, nr, share, width),
        block,
        left.reshape(2, m, piece, width),
        relations.reshape(nl, nr, share, width),
    )
    return (
        left_next.reshape(ent_l, width), moved, relations_next.reshape(rels, width),
    )


def solution(mesh):
    nl, nr = mesh.shape["left"], mesh.shape["right"]

    def shards(left, right, relations, src, kind, dst, neg, count):
        lgrad, rgrad, block = terms(
            left, right[0], relations, src[0], kind[0], dst[0], neg[0, 0], count
        )
        left_next, moved, relations_next = exchange(
            nl, nr, lgrad, rgrad, block, left, relations
        )
        return (left_next, moved[None], relations_next)

    return jax.shard_map(
        shards,
        mesh=mesh,
        in_specs=(
            P("left", None),
            P("left", "right", None),
            P(),
            P("left", "right", None),
            P("left", "right", None),
            P("left", "right", None),
            P("left", "right", None, None),
            P("left", "right"),
        ),
        out_specs=(P("left", None), P("left", "right", None), P()),
        check_vma=False,
    )
```

```python
import functools

import jax
import jax.numpy as jnp
from jax import lax
from jax.experimental import pallas as pl
from jax.experimental.pallas import tpu as pltpu
from jax.sharding import PartitionSpec as P

step_size = 0.5
relation_step = 12.0

f32, bf16 = jnp.float32, jnp.bfloat16
VMEM = pltpu.VMEM


def split(value):
    high = value.astype(bf16)
    low = (value - high.astype(f32)).astype(bf16)
    return jnp.concatenate([high, low], axis=1)


def joined(value):
    half = value.shape[1] // 2
    return value[:, :half] + value[:, half:]


def matmul(a, b, dims=((1,), (0,))):
    return lax.dot_general(a, b, (dims, ((), ())), preferred_element_type=f32)


def one_hot(ids, shape, axis):
    place = lax.broadcasted_iota(jnp.int32, shape, axis)
    return jnp.where(place == ids, 1.0, 0.0).astype(bf16)


def low_bit(mask):
    return (mask & -mask).bit_length() - 1


def flip(value, mask):
    bit = 1
    while bit <= mask:
        if mask & bit:
            value = value + bit * (1 - 2 * lax.rem(value // bit, 2))
        bit *= 2
    return value


def round_kernel(
    nl, nr,
    count_ref, left_any, right_any, rel_any, src_any, kind_any, dst_any, neg_any,
    left_out, block_out, rel_out,
    left_ref, right_ref, rel_ref, src_ref, kind_ref, dst_ref, neg_ref,
    rows_ref, cols_ref, rel_parts, neg_parts, heads, kinds, tails, low_ref, weights,
    block_ref, to_mate, held, pair_in, level_in, rgrad, rel_in, rel_mid, rel_part,
    load_sems, send_sems, block_recv, pair_recv, level_recv, rows_recv, back_recv,
    ra_recv, rb_recv, rc_recv, rd_recv,
):
    m = nr // 2
    levels = m.bit_length() - 1
    edges = src_ref.shape[1]
    ent_l, width = left_ref.shape
    ent_r = right_ref.shape[0]
    share = rel_ref.shape[2]
    rels = nl * nr * share
    negs = neg_ref.shape[1]
    half = width // 2
    piece = ent_l // nr
    block = min(256, edges)
    l, r = lax.axis_index("left"), lax.axis_index("right")
    line, side = r // 2, lax.rem(r, 2)
    mate = line * 2 + (1 - side)

    loads = []
    for i, (src, dst) in enumerate((
        (src_any, src_ref), (kind_any, kind_ref), (dst_any, dst_ref), (neg_any, neg_ref),
        (rel_any, rel_ref), (right_any, right_ref), (left_any, left_ref),
    )):
        load = pltpu.make_async_copy(src, dst, load_sems.at[i])
        load.start()
        loads.append(load)

    def across(src, dst, send, recv, axis, to):
        return pltpu.make_async_remote_copy(
            src_ref=src, dst_ref=dst, send_sem=send, recv_sem=recv,
            device_id={axis: to}, device_id_type=pl.DeviceIdType.MESH,
        )

    def others(me, count):
        return [lax.rem(me + k, count) for k in range(1, count)]

    lefts, rights = others(l, nl), others(r, nr)

    barrier = pltpu.get_barrier_semaphore()
    for axis, peers in (("left", lefts), ("right", rights)):
        for peer in peers:
            pl.semaphore_signal(
                barrier, inc=1, device_id={axis: peer},
                device_id_type=pl.DeviceIdType.MESH,
            )

    for load in loads:
        load.wait()

    rows_ref[...] = jnp.zeros_like(rows_ref)
    rows_ref[0:1, :] = src_ref[...]
    rows_ref[1:2, :] = kind_ref[...]
    rows_ref[2:3, :] = dst_ref[...]
    cols_ref[...] = jnp.transpose(rows_ref[...])
    rel_parts[...] = split(rel_ref[...].reshape(rels, width))
    place = lax.broadcasted_iota(jnp.int32, (ent_r, negs), 0)
    times = jnp.sum(jnp.where(place == neg_ref[...], 1.0, 0.0), axis=1, keepdims=True)
    neg_parts[...] = split(right_ref[...].astype(f32) * times)
    count = count_ref[0, 0]

    @pl.loop(0, edges // block)
    def _(step):
        start = pl.multiple_of(step * block, block)
        here = pl.ds(start, block)
        ids = cols_ref[here, :]
        head = matmul(one_hot(ids[:, 0:1], (block, ent_l), 1), left_ref[...])
        rel = joined(matmul(one_hot(ids[:, 1:2], (block, rels), 1), rel_parts[...]))
        tail = matmul(one_hot(ids[:, 2:3], (block, ent_r), 1), right_ref[...])
        slot = start + lax.broadcasted_iota(jnp.int32, (block, 1), 0)
        live = jnp.where(slot < count, 1.0, 0.0)
        hre, him = head[:, :half], head[:, half:]
        rre, rim = rel[:, :half], rel[:, half:]
        query = jnp.concatenate([hre * rre - him * rim, hre * rim + him * rre], axis=1)
        q_low = query.astype(bf16)
        pos = jnp.sum(query * tail, axis=1, keepdims=True)
        scores = matmul(q_low, right_ref[...], ((1,), (1,)))
        c_pos = -live / (1.0 + jnp.exp(pos))
        c_neg = ((live / negs) / (1.0 + jnp.exp(-scores))).astype(bf16)
        g_query = joined(matmul(c_neg, neg_parts[...])) + c_pos * tail
        gre, gim = g_query[:, :half], g_query[:, half:]
        heads[here, :] = split(
            jnp.concatenate([gre * rre + gim * rim, -gre * rim + gim * rre], axis=1)
        )
        kinds[here, :] = split(
            jnp.concatenate([gre * hre + gim * him, -gre * him + gim * hre], axis=1)
        )
        tails[here, :] = split(c_pos * query)
        low_ref[here, :] = q_low
        weights[here, :] = c_neg

    def summed(ids_row, start, size, parts):
        hot = one_hot(ids_row[...] - start, (size, edges), 0)
        return joined(matmul(hot, parts[...]))

    pl.semaphore_wait(barrier, nl - 1 + nr - 1)

    started = []

    def start(src, dst, recv, axis, to):
        copy = across(src, dst, send_sems.at[len(started)], recv, axis, to)
        copy.start()
        started.append(copy)

    def arrived(dst, sem, axis="right"):
        across(dst, dst, sem, sem, axis, mate if axis == "right" else lefts[0]).wait_recv()

    for peer in lefts:
        rgrad[peer] = summed(kind_ref, peer * (nr * share), nr * share, kinds).reshape(
            nr, share, width
        )
        start(rgrad.at[peer], rel_in.at[l], ra_recv.at[l], "left", peer)

    order = list(range(m - 1, -1, -1))
    spots = [flip(line, k) for k in range(m)]
    for k in order:
        to_mate[k] = summed(src_ref, ((1 - side) * m + spots[k]) * piece, piece, heads)
        start(to_mate.at[k], pair_in.at[k], pair_recv.at[k], "right", mate)

    total = summed(kind_ref, l * (nr * share), nr * share, kinds).reshape(nr, share, width)
    for peer in lefts:
        arrived(rel_in.at[peer], ra_recv.at[peer], "left")
        total = total + rel_in[peer]
    rel_part[...] = total
    for peer in rights:
        start(rel_part.at[peer], rel_mid.at[r], rb_recv.at[r], "right", peer)

    for k in order:
        held[k] = summed(src_ref, (side * m + spots[k]) * piece, piece, heads)

    grad = matmul(weights[...], low_ref[...], ((0,), (0,))) * times
    hot = one_hot(dst_ref[...], (ent_r, edges), 0)
    grad = grad + joined(matmul(hot, tails[...]))
    block_ref[...] = (right_ref[...].astype(f32) - step_size * grad).astype(bf16)
    start(block_ref, block_out, block_recv.at[0], "right", lax.rem(r + 1, nr))

    for k in order:
        arrived(pair_in.at[k], pair_recv.at[k])
        total = held[k] + pair_in[k]
        top = low_bit(k) if k else levels
        for level in range(top):
            arrived(level_in.at[level, k], level_recv.at[level, k])
            total = total + level_in[level, k]
        if k:
            held[k] = total
            there = k - (1 << top)
            start(
                held.at[k], level_in.at[top, there], level_recv.at[top, there],
                "right", spots[1 << top] * 2 + side,
            )
    own_rows = pl.ds(pl.multiple_of((side * m + line) * piece, piece), piece)
    left_out[side, line] = (
        left_ref[own_rows, :].astype(f32) - step_size * total
    ).astype(bf16)

    def pass_on(k):
        rows = left_out.at[side, spots[k]]
        for level in range((low_bit(k) if k else levels) - 1, -1, -1):
            there = k + (1 << level)
            start(rows, rows, rows_recv.at[there], "right", spots[1 << level] * 2 + side)
        start(rows, rows, back_recv.at[k], "right", mate)

    pass_on(0)

    total = rel_part[r]
    for peer in rights:
        arrived(rel_mid.at[peer], rb_recv.at[peer])
        total = total + rel_mid[peer]
    rel_out[l, r] = rel_ref[l, r] - relation_step * total
    for peer in rights:
        start(rel_out.at[l, r], rel_out.at[l, r], rc_recv.at[r], "right", peer)

    later = sorted(range(1, m), key=lambda k: (-low_bit(k), k))
    for k in later[:1]:
        arrived(left_out.at[side, spots[k]], rows_recv.at[k])
        pass_on(k)
    for peer in rights:
        arrived(rel_out.at[l, peer], rc_recv.at[peer])
    for peer in lefts:
        start(rel_out.at[l], rel_out.at[l], rd_recv.at[l], "left", peer)
    for k in later[1:]:
        arrived(left_out.at[side, spots[k]], rows_recv.at[k])
        pass_on(k)

    for k in [0] + later:
        arrived(left_out.at[1 - side, spots[k]], back_recv.at[k])
    for peer in lefts:
        arrived(rel_out.at[peer], rd_recv.at[peer], "left")
    arrived(block_out, block_recv.at[0])
    for copy in started:
        copy.wait_send()


def bucket_round(nl, nr, left, right, relations, src, kind, dst, neg, count):
    m = nr // 2
    levels = max(m.bit_length() - 1, 1)
    edges, negs = src.shape[1], neg.shape[1]
    ent_l, width = left.shape
    ent_r, rels = right.shape[0], relations.shape[0]
    piece, share = ent_l // nr, rels // (nl * nr)
    whole = pl.BlockSpec(memory_space=VMEM)
    outside = pl.BlockSpec(memory_space=pl.ANY)
    dma = pltpu.SemaphoreType.DMA
    sends = 2 * (nl - 1) + 2 * (nr - 1) + 1 + m + (m - 1) + (m - 1) + m
    left_next, moved, relations_next = pl.pallas_call(
        functools.partial(round_kernel, nl, nr),
        out_shape=(
            jax.ShapeDtypeStruct((2, m, piece, width), bf16),
            jax.ShapeDtypeStruct((ent_r, width), bf16),
            jax.ShapeDtypeStruct((nl, nr, share, width), f32),
        ),
        in_specs=[pl.BlockSpec(memory_space=pltpu.SMEM)] + [outside] * 7,
        out_specs=(whole,) * 3,
        scratch_shapes=[
            VMEM((ent_l, width), bf16),
            VMEM((ent_r, width), bf16),
            VMEM((nl, nr, share, width), f32),
            VMEM((1, edges), jnp.int32),
            VMEM((1, edges), jnp.int32),
            VMEM((1, edges), jnp.int32),
            VMEM((1, negs), jnp.int32),
            VMEM((8, edges), jnp.int32),
            VMEM((edges, 8), jnp.int32),
            VMEM((rels, 2 * width), bf16),
            VMEM((ent_r, 2 * width), bf16),
            VMEM((edges, 2 * width), bf16),
            VMEM((edges, 2 * width), bf16),
            VMEM((edges, 2 * width), bf16),
            VMEM((edges, width), bf16),
            VMEM((edges, ent_r), bf16),
            VMEM((ent_r, width), bf16),
            VMEM((m, piece, width), f32),
            VMEM((m, piece, width), f32),
            VMEM((m, piece, width), f32),
            VMEM((levels, m, piece, width), f32),
            VMEM((nl, nr, share, width), f32),
            VMEM((nl, nr, share, width), f32),
            VMEM((nr, share, width), f32),
            VMEM((nr, share, width), f32),
            dma((7,)), dma((sends,)), dma((1,)), dma((m,)), dma((levels, m)),
            dma((m,)), dma((m,)), dma((nl,)), dma((nr,)), dma((nr,)), dma((nl,)),
        ],
        compiler_params=pltpu.CompilerParams(
            collective_id=0, has_side_effects=True, vmem_limit_bytes=44 * 2**20
        ),
        name="bucket_round",
    )(
        count, left, right, relations.reshape(nl, nr, share, width), src, kind, dst, neg,
    )
    return (
        left_next.reshape(ent_l, width), moved, relations_next.reshape(rels, width),
    )


def solution(mesh):
    nl, nr = mesh.shape["left"], mesh.shape["right"]

    def shards(left, right, relations, src, kind, dst, neg, count):
        left_next, moved, relations_next = bucket_round(
            nl, nr, left, right[0], relations, src[0], kind[0], dst[0], neg[0, 0], count
        )
        return (left_next, moved[None], relations_next)

    return jax.shard_map(
        shards,
        mesh=mesh,
        in_specs=(
            P("left", None),
            P("left", "right", None),
            P(),
            P("left", "right", None),
            P("left", "right", None),
            P("left", "right", None),
            P("left", "right", None, None),
            P("left", "right"),
        ),
        out_specs=(P("left", None), P("left", "right", None), P()),
        check_vma=False,
    )
```

```python
import functools

import jax
import jax.numpy as jnp
from jax import lax
from jax.experimental import pallas as pl
from jax.experimental.pallas import tpu as pltpu
from jax.sharding import PartitionSpec as P

step_size = 0.5
relation_step = 12.0
PARTS = 2

f32, bf16 = jnp.float32, jnp.bfloat16
VMEM = pltpu.VMEM


def split(value):
    high = value.astype(bf16)
    low = (value - high.astype(f32)).astype(bf16)
    return jnp.concatenate([high, low], axis=1)


def joined(value):
    half = value.shape[1] // 2
    return value[:, :half] + value[:, half:]


def matmul(a, b, dims=((1,), (0,))):
    return lax.dot_general(a, b, (dims, ((), ())), preferred_element_type=f32)


def one_hot(ids, shape, axis):
    place = lax.broadcasted_iota(jnp.int32, shape, axis)
    return jnp.where(place == ids, 1.0, 0.0).astype(bf16)


def low_bit(mask):
    return (mask & -mask).bit_length() - 1


def flip(value, mask):
    bit = 1
    while bit <= mask:
        if mask & bit:
            value = value + bit * (1 - 2 * lax.rem(value // bit, 2))
        bit *= 2
    return value


def round_kernel(
    nl, nr, parts,
    count_ref, left_any, right_any, rel_any, src_any, kind_any, dst_any, neg_any,
    left_out, block_out, rel_out,
    left_ref, right_ref, rel_ref, src_ref, kind_ref, dst_ref, neg_ref,
    rows_ref, cols_ref, rel_parts, neg_parts, heads, kinds, tails, low_ref, weights,
    block_ref, to_mate, held, pair_in, level_in, rgrad, rel_in, rel_mid, rel_part,
    load_sems, send_sems, block_recv, pair_recv, level_recv, rows_recv, back_recv,
    ra_recv, rb_recv, rc_recv, rd_recv,
):
    m = nr // 2
    levels = m.bit_length() - 1
    edges = src_ref.shape[1]
    ent_l, width = left_ref.shape
    ent_r = right_ref.shape[0]
    share = rel_ref.shape[2]
    rels = nl * nr * share
    negs = neg_ref.shape[1]
    half = width // 2
    piece = ent_l // nr
    sub = piece // parts
    block = min(256, edges)
    l, r = lax.axis_index("left"), lax.axis_index("right")
    line, side = r // 2, lax.rem(r, 2)
    mate = line * 2 + (1 - side)

    loads = []
    for i, (src, dst) in enumerate((
        (src_any, src_ref), (kind_any, kind_ref), (dst_any, dst_ref), (neg_any, neg_ref),
        (rel_any, rel_ref), (right_any, right_ref), (left_any, left_ref),
    )):
        load = pltpu.make_async_copy(src, dst, load_sems.at[i])
        load.start()
        loads.append(load)

    def across(src, dst, send, recv, axis, to):
        return pltpu.make_async_remote_copy(
            src_ref=src, dst_ref=dst, send_sem=send, recv_sem=recv,
            device_id={axis: to}, device_id_type=pl.DeviceIdType.MESH,
        )

    def others(me, count):
        return [lax.rem(me + k, count) for k in range(1, count)]

    lefts, rights = others(l, nl), others(r, nr)

    barrier = pltpu.get_barrier_semaphore()
    for axis, peers in (("left", lefts), ("right", rights)):
        for peer in peers:
            pl.semaphore_signal(
                barrier, inc=1, device_id={axis: peer},
                device_id_type=pl.DeviceIdType.MESH,
            )

    for load in loads:
        load.wait()

    rows_ref[...] = jnp.zeros_like(rows_ref)
    rows_ref[0:1, :] = src_ref[...]
    rows_ref[1:2, :] = kind_ref[...]
    rows_ref[2:3, :] = dst_ref[...]
    cols_ref[...] = jnp.transpose(rows_ref[...])
    rel_parts[...] = split(rel_ref[...].reshape(rels, width))
    place = lax.broadcasted_iota(jnp.int32, (ent_r, negs), 0)
    times = jnp.sum(jnp.where(place == neg_ref[...], 1.0, 0.0), axis=1, keepdims=True)
    neg_parts[...] = split(right_ref[...].astype(f32) * times)
    count = count_ref[0, 0]

    @pl.loop(0, edges // block)
    def _(step):
        start = pl.multiple_of(step * block, block)
        here = pl.ds(start, block)
        ids = cols_ref[here, :]
        head = matmul(one_hot(ids[:, 0:1], (block, ent_l), 1), left_ref[...])
        rel = joined(matmul(one_hot(ids[:, 1:2], (block, rels), 1), rel_parts[...]))
        tail = matmul(one_hot(ids[:, 2:3], (block, ent_r), 1), right_ref[...])
        slot = start + lax.broadcasted_iota(jnp.int32, (block, 1), 0)
        live = jnp.where(slot < count, 1.0, 0.0)
        hre, him = head[:, :half], head[:, half:]
        rre, rim = rel[:, :half], rel[:, half:]
        query = jnp.concatenate([hre * rre - him * rim, hre * rim + him * rre], axis=1)
        q_low = query.astype(bf16)
        pos = jnp.sum(query * tail, axis=1, keepdims=True)
        scores = matmul(q_low, right_ref[...], ((1,), (1,)))
        c_pos = -live / (1.0 + jnp.exp(pos))
        c_neg = ((live / negs) / (1.0 + jnp.exp(-scores))).astype(bf16)
        g_query = joined(matmul(c_neg, neg_parts[...])) + c_pos * tail
        gre, gim = g_query[:, :half], g_query[:, half:]
        heads[here, :] = split(
            jnp.concatenate([gre * rre + gim * rim, -gre * rim + gim * rre], axis=1)
        )
        kinds[here, :] = split(
            jnp.concatenate([gre * hre + gim * him, -gre * him + gim * hre], axis=1)
        )
        tails[here, :] = split(c_pos * query)
        low_ref[here, :] = q_low
        weights[here, :] = c_neg

    def summed(ids_row, start, size, parts):
        hot = one_hot(ids_row[...] - start, (size, edges), 0)
        return joined(matmul(hot, parts[...]))

    pl.semaphore_wait(barrier, nl - 1 + nr - 1)

    started = []

    def start(src, dst, recv, axis, to):
        copy = across(src, dst, send_sems.at[len(started)], recv, axis, to)
        copy.start()
        started.append(copy)

    def arrived(dst, sem, axis="right"):
        across(dst, dst, sem, sem, axis, mate if axis == "right" else lefts[0]).wait_recv()

    order = list(range(m - 1, -1, -1))
    later = sorted(range(1, m), key=lambda k: (-low_bit(k), k))
    spots = [flip(line, k) for k in range(m)]

    def left_rows(which, c, k):
        return summed(src_ref, (which * m + spots[k]) * piece + c * sub, sub, heads)

    def to_the_mate(c):
        for k in order:
            to_mate[c, k] = left_rows(1 - side, c, k)
            start(to_mate.at[c, k], pair_in.at[c, k], pair_recv.at[c, k], "right", mate)

    to_the_mate(0)

    for peer in lefts:
        rgrad[peer] = summed(kind_ref, peer * (nr * share), nr * share, kinds).reshape(
            nr, share, width
        )
        start(rgrad.at[peer], rel_in.at[l], ra_recv.at[l], "left", peer)

    for c in range(1, parts):
        to_the_mate(c)
    for k in order:
        held[0, k] = left_rows(side, 0, k)

    total = summed(kind_ref, l * (nr * share), nr * share, kinds).reshape(nr, share, width)
    for peer in lefts:
        arrived(rel_in.at[peer], ra_recv.at[peer], "left")
        total = total + rel_in[peer]
    rel_part[...] = total
    for peer in rights:
        start(rel_part.at[peer], rel_mid.at[r], rb_recv.at[r], "right", peer)

    for c in range(1, parts):
        for k in order:
            held[c, k] = left_rows(side, c, k)

    grad = matmul(weights[...], low_ref[...], ((0,), (0,))) * times
    hot = one_hot(dst_ref[...], (ent_r, edges), 0)
    grad = grad + joined(matmul(hot, tails[...]))
    block_ref[...] = (right_ref[...].astype(f32) - step_size * grad).astype(bf16)

    def rows_of(which, c, k):
        return left_out.at[which, spots[k], pl.ds(c * sub, sub)]

    def pass_on(c, k):
        rows = rows_of(side, c, k)
        for level in range((low_bit(k) if k else levels) - 1, -1, -1):
            there = k + (1 << level)
            start(
                rows, rows, rows_recv.at[c, there], "right",
                spots[1 << level] * 2 + side,
            )
        start(rows, rows, back_recv.at[c, k], "right", mate)

    def forward(c, k):
        arrived(rows_of(side, c, k), rows_recv.at[c, k])
        pass_on(c, k)

    for c in range(parts):
        waiting = list(later) if c else []
        for k in order:
            arrived(pair_in.at[c, k], pair_recv.at[c, k])
            if c == parts - 1 and k == 0:
                start(block_ref, block_out, block_recv.at[0], "right", lax.rem(r + 1, nr))
            total = held[c, k] + pair_in[c, k]
            top = low_bit(k) if k else levels
            for level in range(top):
                arrived(level_in.at[c, level, k], level_recv.at[c, level, k])
                total = total + level_in[c, level, k]
            if k:
                held[c, k] = total
                there = k - (1 << top)
                start(
                    held.at[c, k], level_in.at[c, top, there],
                    level_recv.at[c, top, there], "right", spots[1 << top] * 2 + side,
                )
            if waiting and k < m - 1 and k:
                forward(c - 1, waiting.pop(0))
        first = pl.multiple_of((side * m + line) * piece + c * sub, sub)
        left_out[side, line, pl.ds(c * sub, sub)] = (
            left_ref[pl.ds(first, sub), :].astype(f32) - step_size * total
        ).astype(bf16)
        pass_on(c, 0)
        for k in waiting:
            forward(c - 1, k)

        if c == 0:
            total = rel_part[r]
            for peer in rights:
                arrived(rel_mid.at[peer], rb_recv.at[peer])
                total = total + rel_mid[peer]
            rel_out[l, r] = rel_ref[l, r] - relation_step * total
            for peer in rights:
                start(rel_out.at[l, r], rel_out.at[l, r], rc_recv.at[r], "right", peer)

    for peer in rights:
        arrived(rel_out.at[l, peer], rc_recv.at[peer])
    for peer in lefts:
        start(rel_out.at[l], rel_out.at[l], rd_recv.at[l], "left", peer)
    for k in later:
        forward(parts - 1, k)

    for c in range(parts):
        for k in [0] + later:
            arrived(rows_of(1 - side, c, k), back_recv.at[c, k])
    for peer in lefts:
        arrived(rel_out.at[peer], rd_recv.at[peer], "left")
    arrived(block_out, block_recv.at[0])
    for copy in started:
        copy.wait_send()


def bucket_round(nl, nr, left, right, relations, src, kind, dst, neg, count):
    m = nr // 2
    levels = max(m.bit_length() - 1, 1)
    edges, negs = src.shape[1], neg.shape[1]
    ent_l, width = left.shape
    ent_r, rels = right.shape[0], relations.shape[0]
    piece, share = ent_l // nr, rels // (nl * nr)
    parts = PARTS if piece % (16 * PARTS) == 0 else 1
    sub = piece // parts
    whole = pl.BlockSpec(memory_space=VMEM)
    outside = pl.BlockSpec(memory_space=pl.ANY)
    dma = pltpu.SemaphoreType.DMA
    sends = 2 * (nl - 1) + 2 * (nr - 1) + 1 + parts * (4 * m - 2)
    left_next, moved, relations_next = pl.pallas_call(
        functools.partial(round_kernel, nl, nr, parts),
        out_shape=(
            jax.ShapeDtypeStruct((2, m, piece, width), bf16),
            jax.ShapeDtypeStruct((ent_r, width), bf16),
            jax.ShapeDtypeStruct((nl, nr, share, width), f32),
        ),
        in_specs=[pl.BlockSpec(memory_space=pltpu.SMEM)] + [outside] * 7,
        out_specs=(whole,) * 3,
        scratch_shapes=[
            VMEM((ent_l, width), bf16),
            VMEM((ent_r, width), bf16),
            VMEM((nl, nr, share, width), f32),
            VMEM((1, edges), jnp.int32),
            VMEM((1, edges), jnp.int32),
            VMEM((1, edges), jnp.int32),
            VMEM((1, negs), jnp.int32),
            VMEM((8, edges), jnp.int32),
            VMEM((edges, 8), jnp.int32),
            VMEM((rels, 2 * width), bf16),
            VMEM((ent_r, 2 * width), bf16),
            VMEM((edges, 2 * width), bf16),
            VMEM((edges, 2 * width), bf16),
            VMEM((edges, 2 * width), bf16),
            VMEM((edges, width), bf16),
            VMEM((edges, ent_r), bf16),
            VMEM((ent_r, width), bf16),
            VMEM((parts, m, sub, width), f32),
            VMEM((parts, m, sub, width), f32),
            VMEM((parts, m, sub, width), f32),
            VMEM((parts, levels, m, sub, width), f32),
            VMEM((nl, nr, share, width), f32),
            VMEM((nl, nr, share, width), f32),
            VMEM((nr, share, width), f32),
            VMEM((nr, share, width), f32),
            dma((7,)), dma((sends,)), dma((1,)), dma((parts, m)), dma((parts, levels, m)),
            dma((parts, m)), dma((parts, m)), dma((nl,)), dma((nr,)), dma((nr,)), dma((nl,)),
        ],
        compiler_params=pltpu.CompilerParams(
            collective_id=0, has_side_effects=True, vmem_limit_bytes=44 * 2**20
        ),
        name="bucket_round",
    )(
        count, left, right, relations.reshape(nl, nr, share, width), src, kind, dst, neg,
    )
    return (
        left_next.reshape(ent_l, width), moved, relations_next.reshape(rels, width),
    )


def solution(mesh):
    nl, nr = mesh.shape["left"], mesh.shape["right"]

    def shards(left, right, relations, src, kind, dst, neg, count):
        left_next, moved, relations_next = bucket_round(
            nl, nr, left, right[0], relations, src[0], kind[0], dst[0], neg[0, 0], count
        )
        return (left_next, moved[None], relations_next)

    return jax.shard_map(
        shards,
        mesh=mesh,
        in_specs=(
            P("left", None),
            P("left", "right", None),
            P(),
            P("left", "right", None),
            P("left", "right", None),
            P("left", "right", None),
            P("left", "right", None, None),
            P("left", "right"),
        ),
        out_specs=(P("left", None), P("left", "right", None), P()),
        check_vma=False,
    )
```
